32 devices in a mesh: visit: 8 (over y, x, core), sky: 4 (over z).
Axes of the slice: x: 2, y: 2, z: 4, core: 2. Of those that a mesh axis runs over, the one named last changes fastest.
Arguments:
- image: bfloat16 [8, 384, 2048], P('visit', None, 'sky'), may hold values from -16 to 16
- variance: bfloat16 [8, 384, 2048], P('visit', None, 'sky'), may hold values from 0.25 to 4
- mask_bits: int32 [8, 384, 2048], P('visit', None, 'sky'), may hold values from 0 to 63, as said below
- boxes: int32 [8, 4], P('visit'), may hold values from 0 to 2048, as said below
- row_filters: bfloat16 [20, 41], replicated, may hold values from -1 to 1
- col_filters: bfloat16 [20, 41], replicated, may hold values from -1 to 1
- coeffs: float32 [8, 20, 6], P('visit'), may hold values from -1.25 to 1.25
Outputs:
- coadd: float32 [384, 2048], P('visit', 'sky')
- weight_sum: float32 [384, 2048], P('visit', 'sky')
The draws below stay inside these ranges and needn't reach their ends.
Inputs may be any that keep to these rules, and one draw needn't show every extreme that they name: `mask_bits`: bits 0 to 5 may be set; bits 0, 1 and 2 reject a pixel. `boxes`: for every piece the first row is below the end row and the first column below the end column.
All inputs are finite; a program needn't handle non-finite values.
Results may differ from the reference program's by a relative error of at most 0.0029.
Values may be sent and summed in bfloat16 or wider, within the bound.
A program may use at most 64 MiB of HBM per device.

```python
import math
import jax
import jax.numpy as jnp
from jax import lax

RAD = 20
TAPS = 41
BASIS = 20
TERMS = 6
ROWS_DEV = 48
COLS_DEV = 512
PIECES = 8
H = 384
W = 2048
N_VISIT = 8


def draw_boxes(key, part):
    key_list = jax.random.split(key, 4)
    row_first = jax.random.randint(key_list[0], (PIECES,), 0, H // 4)
    row_end = H - jax.random.randint(key_list[1], (PIECES,), 0, H // 4)
    col_first = jax.random.randint(key_list[2], (PIECES,), 0, W // 4)
    col_end = W - jax.random.randint(key_list[3], (PIECES,), 0, W // 4)
    return jnp.stack([row_first, row_end, col_first, col_end], axis=1).astype(jnp.int32)


def draw_mask_bits(key, part):
    bit_sum = jnp.zeros((PIECES, H, W), jnp.int32)
    for bit_number in range(6):
        hit_mask = jax.random.randint(jax.random.fold_in(key, bit_number), (PIECES, H, W), 0, 16) == 0
        bit_sum = bit_sum + hit_mask.astype(jnp.int32) * 2 ** bit_number
    return bit_sum


def block_scale(own_key, extent, cuts, least, top_value):
    factor_of = 1.0
    for position, shards_of in cuts:
        steps = jax.random.uniform(jax.random.fold_in(jax.random.fold_in(own_key, 6), position), (shards_of,), jnp.float32, least / len(cuts), top_value / len(cuts))
        factor_of = factor_of * jnp.repeat(jnp.exp(steps), extent[position] // shards_of).reshape((-1,) + (1,) * (len(extent) - 1 - position))
    return factor_of


def scatter_about(own_key, extent, deviation, reach, shards=(), kind=jnp.bfloat16):
    level = block_scale(own_key, extent, shards, -0.22, 0.18) if shards else 1.0
    entries = jax.random.normal(own_key, extent, jnp.float32) * deviation * level
    return jnp.minimum(jnp.maximum(entries, -reach), reach).astype(kind)


def setup_inputs(seed: int = 0) -> dict:
    key_of = jax.random.split(jax.random.key(seed), 8)
    return {
        "image": scatter_about(key_of[0], (PIECES, H, W), 3.0, 16.0, ((0, 8), (2, 4))),
        "variance": jnp.clip(jnp.exp(math.log(4.0) - 2.7725887 * jax.random.uniform(key_of[1], (PIECES, H, W), jnp.float32) ** block_scale(key_of[1], (PIECES, H, W), ((0, 8), (2, 4)), -0.2, 0.2)), 0.25, 4.0).astype(jnp.bfloat16),
        "mask_bits": draw_mask_bits(jax.random.fold_in(key_of[7], 71), 0),
        "boxes": draw_boxes(jax.random.fold_in(key_of[7], 71), 0),
        "row_filters": scatter_about(key_of[4], (BASIS, TAPS), TAPS ** -0.5, 1.0),
        "col_filters": scatter_about(key_of[5], (BASIS, TAPS), TAPS ** -0.5, 1.0),
        "coeffs": scatter_about(key_of[6], (PIECES, BASIS, TERMS), BASIS ** -0.5, 1.25, ((0, 8),), jnp.float32),
    }


reject_bits = 7


def toeplitz_stack(filters, out_len, in_len):
    offsets = jnp.arange(in_len, dtype=jnp.int32)[None, :] - jnp.arange(out_len, dtype=jnp.int32)[:, None]
    onehot = (offsets[:, :, None] == jnp.arange(filters.shape[1], dtype=jnp.int32)[None, None, :]).astype(jnp.float32)
    return jnp.einsum("oit,bt->boi", onehot, filters.astype(jnp.float32), precision=lax.Precision.HIGHEST)


def reference(image, variance, mask_bits, boxes, row_filters, col_filters, coeffs):
    height = image.shape[1]
    width = image.shape[2]
    col_block = min(128, COLS_DEV)
    window_rows = ROWS_DEV + 2 * RAD
    row_mats = toeplitz_stack(row_filters, ROWS_DEV, window_rows)
    col_mats = toeplitz_stack(col_filters, col_block, col_block + 2 * RAD)
    row_index = jnp.arange(height, dtype=jnp.int32)[:, None]
    col_index = jnp.arange(width, dtype=jnp.int32)[None, :]
    ycoord = (2.0 * row_index.astype(jnp.float32) + 1.0) / height - 1.0
    xcoord = (2.0 * col_index.astype(jnp.float32) + 1.0) / width - 1.0
    count_blocks = width // col_block

    def one_piece(carry, items):
        picture, spread, bit_plane, piece_box, factors = items
        inside = (row_index >= piece_box[0]) & (row_index < piece_box[1])
        inside = inside & (col_index >= piece_box[2]) & (col_index < piece_box[3])
        inside = inside & (jnp.bitwise_and(bit_plane, reject_bits) == 0)
        masked = jnp.where(inside, spread, jnp.zeros_like(spread))
        positive = masked > 0
        weights = jnp.where(positive, 1.0 / jnp.where(positive, masked, jnp.ones_like(masked)).astype(jnp.float32), jnp.float32(0.0))
        extended = jnp.pad(picture, ((RAD, RAD), (RAD, RAD))).astype(jnp.float32)
        windows = jnp.stack([extended[:, block_id * col_block:block_id * col_block + col_block + 2 * RAD] for block_id in range(count_blocks)], axis=1)

        def basis_step(total, basis_items):
            col_mat, row_mat, poly_terms = basis_items
            colpass = jnp.einsum("rkj,cj->rkc", windows, col_mat, precision=lax.Precision.HIGHEST).astype(jnp.bfloat16)
            colpass = lax.optimization_barrier(colpass).astype(jnp.float32).reshape(height + 2 * RAD, width)
            bands = jnp.stack([colpass[band_id * ROWS_DEV:band_id * ROWS_DEV + window_rows] for band_id in range(N_VISIT)])
            rowpass = jnp.einsum("sr,vrc->vsc", row_mat, bands, precision=lax.Precision.HIGHEST).reshape(height, width)
            coef_field = poly_terms[0] + poly_terms[1] * xcoord + poly_terms[2] * ycoord + poly_terms[3] * (xcoord * xcoord) + poly_terms[4] * (xcoord * ycoord) + poly_terms[5] * (ycoord * ycoord)
            return total + coef_field * rowpass, None

        matched, _ = lax.scan(basis_step, jnp.zeros((height, width), jnp.float32), (col_mats, row_mats, factors))
        running_sum, weight_total = carry
        return (running_sum + weights * matched, weight_total + weights), None

    start_pair = (jnp.zeros((height, width), jnp.float32), jnp.zeros((height, width), jnp.float32))
    (numerator, denominator), _ = lax.scan(one_piece, start_pair, (image, variance, mask_bits, boxes, coeffs))
    return numerator / jnp.maximum(denominator, 1.0), denominator
```

```python
import functools

import jax
import jax.numpy as jnp
from jax import lax
from jax.experimental import pallas as pl
from jax.experimental.pallas import tpu as pltpu
from jax.sharding import PartitionSpec as P

RAD = 20
ROWS_DEV = 48
REJECT = 7
LANES = 128
GROUP = 4
BAND = GROUP * ROWS_DEV
PAD = 32
WIN = BAND + 2 * PAD
MESH = pl.DeviceIdType.MESH


def kernel(
    visits,
    skies,
    image_ref,
    var_ref,
    bits_ref,
    boxes_ref,
    rowf_ref,
    colf_ref,
    coef_ref,
    coadd_ref,
    wsum_ref,
    halo_l,
    halo_r,
    masked,
    got_var,
    matched,
    got_pix,
    total,
    windows,
    row_mats,
    col_mats,
    colpass,
    filt,
    var_send,
    var_recv,
    pix_send,
    pix_recv,
    halo_send,
    halo_recv,
):
    height, cols = image_ref.shape[1], image_ref.shape[2]
    width = cols * skies
    basis, taps = rowf_ref.shape
    blocks = cols // LANES
    groups = visits // GROUP
    v = lax.axis_index("visit")
    z = lax.axis_index("sky")
    my_group = v // GROUP
    has_l = z > 0
    has_r = z < skies - 1

    barrier = pltpu.get_barrier_semaphore()
    for step in range(1, visits):
        pl.semaphore_signal(
            barrier, inc=1, device_id=(lax.rem(v + step, visits), z), device_id_type=MESH
        )

    @pl.when(has_l)
    def _():
        pl.semaphore_signal(barrier, inc=1, device_id=(v, z - 1), device_id_type=MESH)

    @pl.when(has_r)
    def _():
        pl.semaphore_signal(barrier, inc=1, device_id=(v, z + 1), device_id_type=MESH)

    col_first = z * cols
    box = [boxes_ref[0, i] for i in range(4)]
    col_index = col_first + lax.broadcasted_iota(jnp.int32, (ROWS_DEV, cols), 1)
    col_inside = (col_index >= box[2]) & (col_index < box[3])
    row_iota = lax.broadcasted_iota(jnp.int32, (ROWS_DEV, cols), 0)

    def mask_band(band, carry):
        first = pl.multiple_of(band * ROWS_DEV, ROWS_DEV)
        rows = pl.ds(first, ROWS_DEV)
        row_index = first + row_iota
        inside = (row_index >= box[0]) & (row_index < box[1]) & col_inside
        inside = inside & ((bits_ref[0, rows, :] & REJECT) == 0)
        masked[rows, :] = jnp.where(inside, var_ref[0, rows, :].astype(jnp.float32), 0.0).astype(
            jnp.bfloat16
        )
        return carry

    lax.fori_loop(0, visits, mask_band, 0)

    pl.semaphore_wait(barrier, visits - 1 + has_l.astype(jnp.int32) + has_r.astype(jnp.int32))

    send_left = pltpu.make_async_remote_copy(
        src_ref=image_ref.at[0, :, pl.ds(0, LANES)],
        dst_ref=halo_r,
        send_sem=halo_send.at[0],
        recv_sem=halo_recv.at[1],
        device_id=(v, z - 1),
        device_id_type=MESH,
    )
    send_right = pltpu.make_async_remote_copy(
        src_ref=image_ref.at[0, :, pl.ds(cols - LANES, LANES)],
        dst_ref=halo_l,
        send_sem=halo_send.at[1],
        recv_sem=halo_recv.at[0],
        device_id=(v, z + 1),
        device_id_type=MESH,
    )

    @pl.when(has_l)
    def _():
        send_left.start()

    @pl.when(has_r)
    def _():
        send_right.start()

    def band_copy(src, dst, send, recv, dest):
        return pltpu.make_async_remote_copy(
            src_ref=src.at[pl.ds(pl.multiple_of(dest * ROWS_DEV, ROWS_DEV), ROWS_DEV), :],
            dst_ref=dst.at[v],
            send_sem=send.at[dest],
            recv_sem=recv.at[v],
            device_id=(dest, z),
            device_id_type=MESH,
        )

    def var_copy(dest):
        return band_copy(masked, got_var, var_send, var_recv, dest)

    def pix_copy(dest):
        return band_copy(matched, got_pix, pix_send, pix_recv, dest)

    for step in range(1, visits):
        var_copy(lax.rem(v + step, visits)).start()

    filt[...] = jnp.zeros_like(filt)
    filt[0, 0:basis, 0:taps] = rowf_ref[...].astype(jnp.float32)
    filt[1, 0:basis, 0:taps] = colf_ref[...].astype(jnp.float32)
    filt[0] = pltpu.roll(filt[0], PAD - RAD, 1)

    def build(b, carry):
        row = jnp.broadcast_to(filt[0, pl.ds(b, 1), :], (BAND, WIN))
        row_mats[b] = pltpu.roll(row, 0, 1, stride=1, stride_axis=0).astype(jnp.bfloat16)
        col = jnp.broadcast_to(filt[1, pl.ds(b, 1), :], (LANES, 2 * LANES))
        col_mats[b] = pltpu.roll(col, 0, 1, stride=1, stride_axis=0).astype(jnp.bfloat16)
        return carry

    lax.fori_loop(0, basis, build, 0)

    @pl.when(has_l)
    def _():
        send_right_here = pltpu.make_async_remote_copy(
            src_ref=image_ref.at[0, :, pl.ds(0, LANES)],
            dst_ref=halo_l,
            send_sem=halo_send.at[0],
            recv_sem=halo_recv.at[0],
            device_id=(v, z - 1),
            device_id_type=MESH,
        )
        send_right_here.wait_recv()

    @pl.when(jnp.logical_not(has_l))
    def _():
        halo_l[...] = jnp.zeros_like(halo_l)

    @pl.when(has_r)
    def _():
        pltpu.make_async_remote_copy(
            src_ref=image_ref.at[0, :, pl.ds(0, LANES)],
            dst_ref=halo_r,
            send_sem=halo_send.at[1],
            recv_sem=halo_recv.at[1],
            device_id=(v, z + 1),
            device_id_type=MESH,
        ).wait_recv()

    @pl.when(jnp.logical_not(has_r))
    def _():
        halo_r[...] = jnp.zeros_like(halo_r)

    for k in range(blocks):
        windows[k, 0:PAD, :] = jnp.zeros((PAD, 2 * LANES), jnp.bfloat16)
        windows[k, PAD + height : PAD + height + PAD, :] = jnp.zeros((PAD, 2 * LANES), jnp.bfloat16)

    def shift_band(band, carry):
        first = pl.multiple_of(band * ROWS_DEV, ROWS_DEV)
        rows = pl.ds(first, ROWS_DEV)
        wide = jnp.concatenate(
            [halo_l[rows, :], image_ref[0, rows, :], halo_r[rows, :]], axis=1
        ).astype(jnp.float32)
        total_lanes = cols + 2 * LANES
        wide = pltpu.roll(wide, total_lanes - (LANES - RAD), 1).astype(jnp.bfloat16)
        dest = pl.ds(pl.multiple_of(first + PAD, 16), ROWS_DEV)
        for k in range(blocks):
            windows[k, dest, :] = wide[:, k * LANES : (k + 2) * LANES]
        return carry

    lax.fori_loop(0, visits, shift_band, 0)

    col_pos = (col_first + lax.broadcasted_iota(jnp.int32, (1, cols), 1)).astype(jnp.float32)
    xc = (2.0 * col_pos + 1.0) / width - 1.0
    xx = xc * xc
    y_iota = lax.broadcasted_iota(jnp.int32, (BAND, LANES), 0)

    def one_group(step, carry):
        group = lax.rem(my_group + 1 + step, groups)
        first = pl.multiple_of(group * BAND, BAND)
        yc = (2.0 * (first + y_iota).astype(jnp.float32) + 1.0) / height - 1.0
        total[...] = jnp.zeros_like(total)

        def pair_step(p, inner):
            image_win = windows[:, pl.ds(first, WIN), :].reshape(blocks * WIN, 2 * LANES)
            mats = col_mats[pl.ds(2 * p, 2)].reshape(2 * LANES, 2 * LANES)
            passed = lax.dot_general(
                image_win, mats, (((1,), (1,)), ((), ())), preferred_element_type=jnp.float32
            ).astype(jnp.bfloat16)
            for k in range(blocks):
                for h in range(2):
                    colpass[h, :, k * LANES : (k + 1) * LANES] = passed[
                        k * WIN : (k + 1) * WIN, h * LANES : (h + 1) * LANES
                    ]
            parts = []
            for h in range(2):
                b = 2 * p + h
                c = [coef_ref[0, b, t] for t in range(6)]
                rowpass = jnp.dot(row_mats[b], colpass[h], preferred_element_type=jnp.float32)
                in_x = c[0] + c[1] * xc + c[3] * xx
                in_xy = c[2] + c[4] * xc
                in_yy = c[5] * yc
                parts.append((rowpass, in_x, in_xy, in_yy))
            for k in range(blocks):
                lanes = slice(k * LANES, (k + 1) * LANES)
                add = total[:, lanes]
                for rowpass, in_x, in_xy, in_yy in parts:
                    field = in_x[:, lanes] + yc * (in_xy[:, lanes] + in_yy)
                    add = add + field * rowpass[:, lanes]
                total[:, lanes] = add
            return inner

        lax.fori_loop(0, basis // 2, pair_step, 0)
        matched[pl.ds(first, BAND), :] = total[...].astype(jnp.bfloat16)
        for j in range(GROUP):
            dest = group * GROUP + j

            @pl.when(dest != v)
            def _():
                pix_copy(dest).start()

        return carry

    lax.fori_loop(0, groups, one_group, 0)

    own_rows = pl.ds(pl.multiple_of(v * ROWS_DEV, ROWS_DEV), ROWS_DEV)

    def weight_of(plane):
        plane = plane.astype(jnp.float32)
        positive = plane > 0
        return jnp.where(positive, 1.0 / jnp.where(positive, plane, 1.0), 0.0)

    own_first = pl.multiple_of((v - my_group * GROUP) * ROWS_DEV, ROWS_DEV)
    own_weight = weight_of(masked[own_rows, :])
    coadd_ref[...] = own_weight * total[pl.ds(own_first, ROWS_DEV), :]
    wsum_ref[...] = own_weight

    def recv_wait(dst, send, recv, source):
        pltpu.make_async_remote_copy(
            src_ref=masked.at[pl.ds(0, ROWS_DEV), :],
            dst_ref=dst.at[source],
            send_sem=send.at[source],
            recv_sem=recv.at[source],
            device_id=(source, z),
            device_id_type=MESH,
        ).wait_recv()

    def add_source(step, carry):
        source = lax.rem(v + step, visits)
        recv_wait(got_var, var_send, var_recv, source)
        weight = weight_of(got_var[source])
        wsum_ref[...] += weight
        recv_wait(got_pix, pix_send, pix_recv, source)
        coadd_ref[...] += weight * got_pix[source].astype(jnp.float32)
        return carry

    lax.fori_loop(1, visits, add_source, 0)
    coadd_ref[...] = coadd_ref[...] / jnp.maximum(wsum_ref[...], 1.0)

    for step in range(1, visits):
        dest = lax.rem(v + step, visits)
        var_copy(dest).wait_send()
        pix_copy(dest).wait_send()

    @pl.when(has_l)
    def _():
        send_left.wait_send()

    @pl.when(has_r)
    def _():
        send_right.wait_send()


def per_device(image, variance, mask_bits, boxes, row_filters, col_filters, coeffs):
    height, cols = image.shape[1], image.shape[2]
    visits, skies = lax.axis_size("visit"), lax.axis_size("sky")
    basis = row_filters.shape[0]
    blocks = cols // LANES
    vmem = pl.BlockSpec(memory_space=pltpu.VMEM)
    smem = pl.BlockSpec(memory_space=pltpu.SMEM)
    band = jax.ShapeDtypeStruct((ROWS_DEV, cols), jnp.float32)
    bf16 = jnp.bfloat16
    dma = pltpu.SemaphoreType.DMA
    return pl.pallas_call(
        functools.partial(kernel, visits, skies),
        out_shape=(band, band),
        in_specs=[vmem, vmem, vmem, smem, vmem, vmem, smem],
        out_specs=(vmem, vmem),
        scratch_shapes=[
            pltpu.VMEM((height, LANES), bf16),
            pltpu.VMEM((height, LANES), bf16),
            pltpu.VMEM((height, cols), bf16),
            pltpu.VMEM((visits, ROWS_DEV, cols), bf16),
            pltpu.VMEM((height, cols), bf16),
            pltpu.VMEM((visits, ROWS_DEV, cols), bf16),
            pltpu.VMEM((BAND, cols), jnp.float32),
            pltpu.VMEM((blocks, height + 2 * PAD, 2 * LANES), bf16),
            pltpu.VMEM((basis, BAND, WIN), bf16),
            pltpu.VMEM((basis, LANES, 2 * LANES), bf16),
            pltpu.VMEM((2, WIN, cols), bf16),
            pltpu.VMEM((2, 24, WIN), jnp.float32),
            dma((visits,)),
            dma((visits,)),
            dma((visits,)),
            dma((visits,)),
            dma((2,)),
            dma((2,)),
        ],
        compiler_params=pltpu.CompilerParams(
            collective_id=0, has_side_effects=True, vmem_limit_bytes=40 * 1024 * 1024
        ),
    )(image, variance, mask_bits, boxes, row_filters, col_filters, coeffs)


def solution(mesh):
    in_specs = (
        P("visit", None, "sky"),
        P("visit", None, "sky"),
        P("visit", None, "sky"),
        P("visit", None),
        P(),
        P(),
        P("visit", None, None),
    )
    out_specs = (P("visit", "sky"), P("visit", "sky"))
    return jax.shard_map(
        per_device, mesh=mesh, in_specs=in_specs, out_specs=out_specs, check_vma=False
    )
```

```python
import functools

import jax
import jax.numpy as jnp
from jax import lax
from jax.experimental import pallas as pl
from jax.experimental.pallas import tpu as pltpu
from jax.sharding import PartitionSpec as P

RAD = 20
ROWS_DEV = 48
REJECT = 7
LANES = 128
GROUP = 4
BAND = GROUP * ROWS_DEV
PAD = 32
WIN = BAND + 2 * PAD
UNITS = 2
MESH = pl.DeviceIdType.MESH


def kernel(
    visits,
    skies,
    image_hbm,
    var_hbm,
    bits_hbm,
    boxes_hbm,
    rowf_hbm,
    colf_hbm,
    coef_hbm,
    sums_ref,
    image_ref,
    var_ref,
    bits_ref,
    boxes_ref,
    rowf_ref,
    colf_ref,
    coef_ref,
    halo_l,
    halo_r,
    masked,
    got_var,
    matched,
    got_pix,
    total,
    windows,
    row_mats,
    col_mats,
    pass_a,
    pass_b,
    filt,
    load_sem,
    var_send,
    var_recv,
    pix_send,
    pix_recv,
    halo_send,
    halo_recv,
):
    height, cols = image_ref.shape[1], image_ref.shape[2]
    width = cols * skies
    basis, taps = rowf_ref.shape
    blocks = cols // LANES
    per_unit = blocks // UNITS
    span = per_unit * LANES
    order = list(range(1, blocks - 1)) + [0, blocks - 1]
    groups = visits // GROUP
    v = lax.axis_index("visit")
    z = lax.axis_index("sky")
    my_group = v // GROUP
    has_l = z > 0
    has_r = z < skies - 1

    barrier = pltpu.get_barrier_semaphore()
    for step in range(1, visits):
        pl.semaphore_signal(
            barrier, inc=1, device_id=(lax.rem(v + step, visits), z), device_id_type=MESH
        )

    @pl.when(has_l)
    def _():
        pl.semaphore_signal(barrier, inc=1, device_id=(v, z - 1), device_id_type=MESH)

    @pl.when(has_r)
    def _():
        pl.semaphore_signal(barrier, inc=1, device_id=(v, z + 1), device_id_type=MESH)

    pairs = (
        (boxes_hbm, boxes_ref),
        (var_hbm, var_ref),
        (bits_hbm, bits_ref),
        (rowf_hbm, rowf_ref),
        (colf_hbm, colf_ref),
        (image_hbm, image_ref),
        (coef_hbm, coef_ref),
    )
    loads = [
        pltpu.make_async_copy(src, dst, load_sem.at[n]) for n, (src, dst) in enumerate(pairs)
    ]
    for load in loads:
        load.start()

    for load in loads[:3]:
        load.wait()
    col_first = z * cols
    box = [boxes_ref[0, i] for i in range(4)]
    col_index = col_first + lax.broadcasted_iota(jnp.int32, (ROWS_DEV, cols), 1)
    col_inside = (col_index >= box[2]) & (col_index < box[3])
    row_iota = lax.broadcasted_iota(jnp.int32, (ROWS_DEV, cols), 0)

    def mask_band(band, carry):
        first = pl.multiple_of(band * ROWS_DEV, ROWS_DEV)
        rows = pl.ds(first, ROWS_DEV)
        row_index = first + row_iota
        inside = (row_index >= box[0]) & (row_index < box[1]) & col_inside
        inside = inside & ((bits_ref[0, rows, :] & REJECT) == 0)
        masked[rows, :] = jnp.where(inside, var_ref[0, rows, :].astype(jnp.float32), 0.0).astype(
            jnp.bfloat16
        )
        return carry

    lax.fori_loop(0, visits, mask_band, 0)

    pl.semaphore_wait(barrier, visits - 1 + has_l.astype(jnp.int32) + has_r.astype(jnp.int32))

    def halo_copy(first, dst, send, recv, target):
        return pltpu.make_async_remote_copy(
            src_ref=image_hbm.at[0, :, pl.ds(first, LANES)],
            dst_ref=dst,
            send_sem=halo_send.at[send],
            recv_sem=halo_recv.at[recv],
            device_id=(v, target),
            device_id_type=MESH,
        )

    @pl.when(has_l)
    def _():
        halo_copy(0, halo_r, 0, 1, z - 1).start()

    @pl.when(has_r)
    def _():
        halo_copy(cols - LANES, halo_l, 1, 0, z + 1).start()

    def rows_of(dest):
        return pl.ds(pl.multiple_of(dest * ROWS_DEV, ROWS_DEV), ROWS_DEV)

    def var_copy(dest, source):
        return pltpu.make_async_remote_copy(
            src_ref=masked.at[rows_of(dest), :],
            dst_ref=got_var.at[source],
            send_sem=var_send.at[dest],
            recv_sem=var_recv.at[source],
            device_id=(dest, z),
            device_id_type=MESH,
        )

    def pix_copy(unit, dest, source):
        return pltpu.make_async_remote_copy(
            src_ref=matched.at[unit, rows_of(dest), :],
            dst_ref=got_pix.at[unit, source],
            send_sem=pix_send.at[unit, dest],
            recv_sem=pix_recv.at[unit, source],
            device_id=(dest, z),
            device_id_type=MESH,
        )

    for step in range(1, visits):
        dest = lax.rem(v + step, visits)
        var_copy(dest, v).start()

    filt[...] = jnp.zeros_like(filt)
    loads[3].wait()
    loads[4].wait()
    filt[0, 0:basis, 0:taps] = rowf_ref[...].astype(jnp.float32)
    filt[1, 0:basis, 0:taps] = colf_ref[...].astype(jnp.float32)
    filt[0] = pltpu.roll(filt[0], PAD - RAD, 1)

    def build(b):
        row = jnp.broadcast_to(filt[0, pl.ds(b, 1), :], (BAND, WIN))
        row_mats[b] = pltpu.roll(row, 0, 1, stride=1, stride_axis=0).astype(jnp.bfloat16)
        col = jnp.broadcast_to(filt[1, pl.ds(b, 1), :], (LANES, 2 * LANES))
        col_mats[b] = pltpu.roll(col, 0, 1, stride=1, stride_axis=0).astype(jnp.bfloat16)

    for k in range(blocks):
        windows[k, 0:PAD, :] = jnp.zeros((PAD, 2 * LANES), jnp.bfloat16)
        windows[k, PAD + height : PAD + height + PAD, :] = jnp.zeros((PAD, 2 * LANES), jnp.bfloat16)

    def shifted(parts, lanes):
        wide = jnp.concatenate(parts, axis=1).astype(jnp.float32)
        back = wide.shape[1] - (LANES - RAD)
        return pltpu.roll(wide, back, 1)[:, :lanes].astype(jnp.bfloat16)

    def window_rows(first):
        return pl.ds(pl.multiple_of(first + PAD, 16), ROWS_DEV)

    def inner_band(band, carry):
        first = pl.multiple_of(band * ROWS_DEV, ROWS_DEV)
        wide = shifted([image_ref[0, pl.ds(first, ROWS_DEV), :]], cols - LANES)
        for k in range(blocks - 2):
            windows[k, window_rows(first), :] = wide[:, k * LANES : (k + 2) * LANES]
        return carry

    def outer_band(band, carry):
        first = pl.multiple_of(band * ROWS_DEV, ROWS_DEV)
        rows = pl.ds(first, ROWS_DEV)
        left = shifted([halo_l[rows, :], image_ref[0, rows, 0 : 2 * LANES]], 2 * LANES)
        windows[blocks - 2, window_rows(first), :] = left
        right = shifted([image_ref[0, rows, cols - 2 * LANES : cols], halo_r[rows, :]], 2 * LANES)
        windows[blocks - 1, window_rows(first), :] = right
        return carry

    loads[5].wait()
    loads[6].wait()
    lax.fori_loop(0, visits, inner_band, 0)

    lane = lax.broadcasted_iota(jnp.int32, (1, LANES), 1)
    y_iota = lax.broadcasted_iota(jnp.int32, (BAND, LANES), 0)

    def one_unit(unit, group, prepare=False):
        first = pl.multiple_of(group * BAND, BAND)
        yc = (2.0 * (first + y_iota).astype(jnp.float32) + 1.0) / height - 1.0
        mine = order[unit * per_unit : (unit + 1) * per_unit]
        xs = []
        for k in mine:
            col_pos = (col_first + k * LANES + lane).astype(jnp.float32)
            xs.append((2.0 * col_pos + 1.0) / width - 1.0)
        total[unit] = jnp.zeros((BAND, span), jnp.float32)

        def col_step(p, passed):
            image_win = windows[unit * per_unit : (unit + 1) * per_unit, pl.ds(first, WIN), :]
            mats = col_mats[pl.ds(2 * p, 2)].reshape(2 * LANES, 2 * LANES)
            out = lax.dot_general(
                image_win.reshape(per_unit * WIN, 2 * LANES),
                mats,
                (((1,), (1,)), ((), ())),
                preferred_element_type=jnp.float32,
            ).astype(jnp.bfloat16)
            for k in range(per_unit):
                for h in range(2):
                    passed[h, :, k * LANES : (k + 1) * LANES] = out[
                        k * WIN : (k + 1) * WIN, h * LANES : (h + 1) * LANES
                    ]

        def row_step(p, passed):
            parts = []
            for h in range(2):
                b = 2 * p + h
                rowpass = jnp.dot(row_mats[b], passed[h], preferred_element_type=jnp.float32)
                parts.append((rowpass, [coef_ref[t, 0, b] for t in range(6)]))
            for k in range(per_unit):
                lanes = slice(k * LANES, (k + 1) * LANES)
                add = total[unit, :, lanes]
                for rowpass, c in parts:
                    in_x = c[0] + c[1] * xs[k] + c[3] * (xs[k] * xs[k])
                    field = in_x + yc * ((c[2] + c[4] * xs[k]) + c[5] * yc)
                    add = add + field * rowpass[:, lanes]
                total[unit, :, lanes] = add

        buffers = (pass_a, pass_b)
        last = basis // 2 - 1
        if prepare:
            build(0)
            build(1)
        col_step(0, buffers[0])
        for p in range(last + 1):
            if prepare and p < last:
                build(2 * p + 2)
                build(2 * p + 3)
            if p < last:
                col_step(p + 1, buffers[(p + 1) % 2])
            row_step(p, buffers[p % 2])
        matched[unit, pl.ds(first, BAND), :] = total[unit].astype(jnp.bfloat16)
        for j in range(GROUP):
            dest = group * GROUP + j

            @pl.when(dest != v)
            def _():
                pix_copy(unit, dest, v).start()

    def group_at(step):
        return lax.rem(my_group + 1 + step, groups)

    one_unit(0, group_at(0), True)

    @pl.when(has_l)
    def _():
        halo_copy(0, halo_l, 0, 0, z - 1).wait_recv()

    @pl.when(has_r)
    def _():
        halo_copy(0, halo_r, 1, 1, z + 1).wait_recv()

    @pl.when(jnp.logical_not(has_l))
    def _():
        halo_l[...] = jnp.zeros_like(halo_l)

    @pl.when(jnp.logical_not(has_r))
    def _():
        halo_r[...] = jnp.zeros_like(halo_r)

    lax.fori_loop(0, visits, outer_band, 0)
    one_unit(1, group_at(0))

    def one_group(step, carry):
        for unit in range(UNITS):
            one_unit(unit, group_at(step))
        return carry

    lax.fori_loop(1, groups, one_group, 0)

    def weight_of(plane):
        plane = plane.astype(jnp.float32)
        positive = plane > 0
        return jnp.where(positive, 1.0 / jnp.where(positive, plane, 1.0), 0.0)

    own_first = pl.multiple_of((v - my_group * GROUP) * ROWS_DEV, ROWS_DEV)
    own_weight = weight_of(masked[rows_of(v), :])
    sums_ref[1] = own_weight

    def in_order(plane_of):
        lanes_of = {}
        for n, k in enumerate(order):
            part = plane_of(n // per_unit)
            at = n % per_unit * LANES
            lanes_of[k] = part[:, at : at + LANES]
        return jnp.concatenate([lanes_of[k] for k in range(blocks)], axis=1)

    sums_ref[0] = own_weight * in_order(lambda unit: total[unit, pl.ds(own_first, ROWS_DEV), :])

    def add_weight(step, carry):
        source = lax.rem(v + step, visits)
        var_copy(source, source).wait_recv()
        sums_ref[1] += weight_of(got_var[source])
        return carry

    lax.fori_loop(1, visits, add_weight, 0)

    base = my_group * GROUP

    def add_source(source):
        for unit in range(UNITS):
            pix_copy(unit, source, source).wait_recv()
        pixels = in_order(lambda unit: got_pix[unit, source]).astype(jnp.float32)
        sums_ref[0] += weight_of(got_var[source]) * pixels

    def add_far(step, carry):
        add_source(lax.rem(base + GROUP + step, visits))
        return carry

    def add_near(step, carry):
        add_source(base + lax.rem(v - base + step, GROUP))
        return carry

    lax.fori_loop(0, visits - GROUP, add_far, 0)
    lax.fori_loop(1, GROUP, add_near, 0)

    for step in range(1, visits):
        dest = lax.rem(v + step, visits)
        var_copy(dest, v).wait_send()
        for unit in range(UNITS):
            pix_copy(unit, dest, v).wait_send()

    @pl.when(has_l)
    def _():
        halo_copy(0, halo_r, 0, 1, z - 1).wait_send()

    @pl.when(has_r)
    def _():
        halo_copy(cols - LANES, halo_l, 1, 0, z + 1).wait_send()


def per_device(image, variance, mask_bits, boxes, row_filters, col_filters, coeffs):
    height, cols = image.shape[1], image.shape[2]
    visits, skies = lax.axis_size("visit"), lax.axis_size("sky")
    basis = row_filters.shape[0]
    blocks = cols // LANES
    span = cols // UNITS
    coeffs = jnp.transpose(coeffs, (2, 0, 1))
    hbm = pl.BlockSpec(memory_space=pltpu.HBM)
    f32, bf16 = jnp.float32, jnp.bfloat16
    dma = pltpu.SemaphoreType.DMA
    sums = pl.pallas_call(
        functools.partial(kernel, visits, skies),
        out_shape=jax.ShapeDtypeStruct((2, ROWS_DEV, cols), f32),
        in_specs=[hbm] * 7,
        out_specs=pl.BlockSpec(memory_space=pltpu.VMEM),
        scratch_shapes=[
            pltpu.VMEM(image.shape, bf16),
            pltpu.VMEM(variance.shape, bf16),
            pltpu.VMEM(mask_bits.shape, jnp.int32),
            pltpu.SMEM(boxes.shape, jnp.int32),
            pltpu.VMEM(row_filters.shape, bf16),
            pltpu.VMEM(col_filters.shape, bf16),
            pltpu.SMEM(coeffs.shape, f32),
            pltpu.VMEM((height, LANES), bf16),
            pltpu.VMEM((height, LANES), bf16),
            pltpu.VMEM((height, cols), bf16),
            pltpu.VMEM((visits, ROWS_DEV, cols), bf16),
            pltpu.VMEM((UNITS, height, span), bf16),
            pltpu.VMEM((UNITS, visits, ROWS_DEV, span), bf16),
            pltpu.VMEM((UNITS, BAND, span), f32),
            pltpu.VMEM((blocks, height + 2 * PAD, 2 * LANES), bf16),
            pltpu.VMEM((basis, BAND, WIN), bf16),
            pltpu.VMEM((basis, LANES, 2 * LANES), bf16),
            pltpu.VMEM((2, WIN, span), bf16),
            pltpu.VMEM((2, WIN, span), bf16),
            pltpu.VMEM((2, 24, WIN), f32),
            dma((7,)),
            dma((visits,)),
            dma((visits,)),
            dma((UNITS, visits)),
            dma((UNITS, visits)),
            dma((2,)),
            dma((2,)),
        ],
        compiler_params=pltpu.CompilerParams(
            collective_id=0, has_side_effects=True, vmem_limit_bytes=62 * 1024 * 1024
        ),
    )(image, variance, mask_bits, boxes, row_filters, col_filters, coeffs)
    return (sums[0] / jnp.maximum(sums[1], 1.0), sums[1])


def solution(mesh):
    in_specs = (
        P("visit", None, "sky"),
        P("visit", None, "sky"),
        P("visit", None, "sky"),
        P("visit", None),
        P(),
        P(),
        P("visit", None, None),
    )
    out_specs = (P("visit", "sky"), P("visit", "sky"))
    return jax.shard_map(
        per_device, mesh=mesh, in_specs=in_specs, out_specs=out_specs, check_vma=False
    )
```

```python
import functools

import jax
import jax.numpy as jnp
from jax import lax
from jax.experimental import pallas as pl
from jax.experimental.pallas import tpu as pltpu
from jax.sharding import PartitionSpec as P

RAD = 20
ROWS_DEV = 48
REJECT = 7
LANES = 128
GROUP = 4
BAND = GROUP * ROWS_DEV
PAD = 32
WIN = BAND + 2 * PAD
UNITS = 2
MESH = pl.DeviceIdType.MESH


def kernel(
    visits,
    skies,
    image_hbm,
    var_hbm,
    bits_hbm,
    boxes_hbm,
    rowf_hbm,
    colf_hbm,
    coef_hbm,
    sums_ref,
    image_ref,
    var_ref,
    bits_ref,
    boxes_ref,
    rowf_ref,
    colf_ref,
    coef_ref,
    halo_l,
    halo_r,
    masked,
    got_var,
    matched,
    got_pix,
    total,
    windows,
    row_mats,
    col_mats,
    pass_a,
    pass_b,
    filt,
    load_sem,
    var_send,
    var_recv,
    pix_send,
    pix_recv,
    halo_send,
    halo_recv,
):
    height, cols = image_ref.shape[1], image_ref.shape[2]
    width = cols * skies
    basis, taps = rowf_ref.shape
    blocks = cols // LANES
    per_unit = blocks // UNITS
    span = per_unit * LANES
    order = list(range(1, blocks - 1)) + [0, blocks - 1]
    groups = visits // GROUP
    few = visits <= 8
    v = lax.axis_index("visit")
    z = lax.axis_index("sky")
    my_group = v // GROUP
    has_l = z > 0
    has_r = z < skies - 1

    barrier = pltpu.get_barrier_semaphore()
    for step in range(1, visits):
        pl.semaphore_signal(
            barrier, inc=1, device_id=(lax.rem(v + step, visits), z), device_id_type=MESH
        )

    @pl.when(has_l)
    def _():
        pl.semaphore_signal(barrier, inc=1, device_id=(v, z - 1), device_id_type=MESH)

    @pl.when(has_r)
    def _():
        pl.semaphore_signal(barrier, inc=1, device_id=(v, z + 1), device_id_type=MESH)

    pairs = (
        (boxes_hbm, boxes_ref),
        (var_hbm, var_ref),
        (bits_hbm, bits_ref),
        (rowf_hbm, rowf_ref),
        (colf_hbm, colf_ref),
        (image_hbm, image_ref),
        (coef_hbm, coef_ref),
    )
    loads = [
        pltpu.make_async_copy(src, dst, load_sem.at[n]) for n, (src, dst) in enumerate(pairs)
    ]
    for load in loads:
        load.start()

    for load in loads[:3]:
        load.wait()
    col_first = z * cols
    box = [boxes_ref[0, i] for i in range(4)]
    col_index = col_first + lax.broadcasted_iota(jnp.int32, (ROWS_DEV, cols), 1)
    col_inside = (col_index >= box[2]) & (col_index < box[3])
    row_iota = lax.broadcasted_iota(jnp.int32, (ROWS_DEV, cols), 0)

    def mask_band(band, carry):
        first = pl.multiple_of(band * ROWS_DEV, ROWS_DEV)
        rows = pl.ds(first, ROWS_DEV)
        row_index = first + row_iota
        inside = (row_index >= box[0]) & (row_index < box[1]) & col_inside
        inside = inside & ((bits_ref[0, rows, :] & REJECT) == 0)
        masked[rows, :] = jnp.where(inside, var_ref[0, rows, :].astype(jnp.float32), 0.0).astype(
            jnp.bfloat16
        )
        return carry

    lax.fori_loop(0, visits, mask_band, 0, unroll=few)

    pl.semaphore_wait(barrier, visits - 1 + has_l.astype(jnp.int32) + has_r.astype(jnp.int32))

    def halo_copy(first, dst, send, recv, target):
        return pltpu.make_async_remote_copy(
            src_ref=image_hbm.at[0, :, pl.ds(first, LANES)],
            dst_ref=dst,
            send_sem=halo_send.at[send],
            recv_sem=halo_recv.at[recv],
            device_id=(v, target),
            device_id_type=MESH,
        )

    @pl.when(has_l)
    def _():
        halo_copy(0, halo_r, 0, 1, z - 1).start()

    @pl.when(has_r)
    def _():
        halo_copy(cols - LANES, halo_l, 1, 0, z + 1).start()

    def rows_of(dest):
        return pl.ds(pl.multiple_of(dest * ROWS_DEV, ROWS_DEV), ROWS_DEV)

    def var_copy(dest, source):
        return pltpu.make_async_remote_copy(
            src_ref=masked.at[rows_of(dest), :],
            dst_ref=got_var.at[source],
            send_sem=var_send.at[dest],
            recv_sem=var_recv.at[source],
            device_id=(dest, z),
            device_id_type=MESH,
        )

    def pix_copy(unit, dest, source):
        return pltpu.make_async_remote_copy(
            src_ref=matched.at[unit, rows_of(dest), :],
            dst_ref=got_pix.at[unit, source],
            send_sem=pix_send.at[unit, dest],
            recv_sem=pix_recv.at[unit, source],
            device_id=(dest, z),
            device_id_type=MESH,
        )

    for step in range(1, visits):
        dest = lax.rem(v + step, visits)
        var_copy(dest, v).start()

    filt[...] = jnp.zeros_like(filt)
    loads[3].wait()
    loads[4].wait()
    filt[0, 0:basis, 0:taps] = rowf_ref[...].astype(jnp.float32)
    filt[1, 0:basis, 0:taps] = colf_ref[...].astype(jnp.float32)
    filt[0] = pltpu.roll(filt[0], PAD - RAD, 1)

    def build(b):
        row = jnp.broadcast_to(filt[0, pl.ds(b, 1), :], (BAND, WIN))
        row_mats[b] = pltpu.roll(row, 0, 1, stride=1, stride_axis=0).astype(jnp.bfloat16)
        col = jnp.broadcast_to(filt[1, pl.ds(b, 1), :], (LANES, 2 * LANES))
        col_mats[b] = pltpu.roll(col, 0, 1, stride=1, stride_axis=0).astype(jnp.bfloat16)

    for k in range(blocks):
        windows[k, 0:PAD, :] = jnp.zeros((PAD, 2 * LANES), jnp.bfloat16)
        windows[k, PAD + height : PAD + height + PAD, :] = jnp.zeros((PAD, 2 * LANES), jnp.bfloat16)

    def shifted(parts, lanes):
        wide = jnp.concatenate(parts, axis=1).astype(jnp.float32)
        back = wide.shape[1] - (LANES - RAD)
        return pltpu.roll(wide, back, 1)[:, :lanes].astype(jnp.bfloat16)

    def window_rows(first):
        return pl.ds(pl.multiple_of(first + PAD, 16), ROWS_DEV)

    def inner_band(band, carry):
        first = pl.multiple_of(band * ROWS_DEV, ROWS_DEV)
        wide = shifted([image_ref[0, pl.ds(first, ROWS_DEV), :]], cols - LANES)
        for k in range(blocks - 2):
            windows[k, window_rows(first), :] = wide[:, k * LANES : (k + 2) * LANES]
        return carry

    def outer_band(band, carry):
        first = pl.multiple_of(band * ROWS_DEV, ROWS_DEV)
        rows = pl.ds(first, ROWS_DEV)
        left = shifted([halo_l[rows, :], image_ref[0, rows, 0 : 2 * LANES]], 2 * LANES)
        windows[blocks - 2, window_rows(first), :] = left
        right = shifted([image_ref[0, rows, cols - 2 * LANES : cols], halo_r[rows, :]], 2 * LANES)
        windows[blocks - 1, window_rows(first), :] = right
        return carry

    loads[5].wait()
    loads[6].wait()
    lax.fori_loop(0, visits, inner_band, 0, unroll=few)

    lane = lax.broadcasted_iota(jnp.int32, (1, LANES), 1)
    y_iota = lax.broadcasted_iota(jnp.int32, (BAND, LANES), 0)

    def one_unit(unit, group, prepare=False):
        first = pl.multiple_of(group * BAND, BAND)
        yc = (2.0 * (first + y_iota).astype(jnp.float32) + 1.0) / height - 1.0
        mine = order[unit * per_unit : (unit + 1) * per_unit]
        xs = []
        for k in mine:
            col_pos = (col_first + k * LANES + lane).astype(jnp.float32)
            xs.append((2.0 * col_pos + 1.0) / width - 1.0)

        def col_step(p, passed):
            image_win = windows[unit * per_unit : (unit + 1) * per_unit, pl.ds(first, WIN), :]
            mats = col_mats[pl.ds(2 * p, 2)].reshape(2 * LANES, 2 * LANES)
            out = lax.dot_general(
                image_win.reshape(per_unit * WIN, 2 * LANES),
                mats,
                (((1,), (1,)), ((), ())),
                preferred_element_type=jnp.float32,
            ).astype(jnp.bfloat16)
            for k in range(per_unit):
                for h in range(2):
                    passed[h, :, k * LANES : (k + 1) * LANES] = out[
                        k * WIN : (k + 1) * WIN, h * LANES : (h + 1) * LANES
                    ]

        def row_step(p, passed):
            parts = []
            for h in range(2):
                b = 2 * p + h
                rowpass = jnp.dot(row_mats[b], passed[h], preferred_element_type=jnp.float32)
                parts.append((rowpass, [coef_ref[t, 0, b] for t in range(6)]))
            for k in range(per_unit):
                lanes = slice(k * LANES, (k + 1) * LANES)
                add = 0.0 if p == 0 else total[unit, :, lanes]
                for rowpass, c in parts:
                    in_x = c[0] + c[1] * xs[k] + c[3] * (xs[k] * xs[k])
                    field = in_x + yc * ((c[2] + c[4] * xs[k]) + c[5] * yc)
                    add = add + field * rowpass[:, lanes]
                total[unit, :, lanes] = add

        buffers = (pass_a, pass_b)
        last = basis // 2 - 1
        if prepare:
            build(0)
            build(1)
        col_step(0, buffers[0])
        for p in range(last + 1):
            if prepare and p < last:
                build(2 * p + 2)
                build(2 * p + 3)
            if p < last:
                col_step(p + 1, buffers[(p + 1) % 2])
            row_step(p, buffers[p % 2])
        matched[unit, pl.ds(first, BAND), :] = total[unit].astype(jnp.bfloat16)
        for j in range(GROUP):
            dest = group * GROUP + j

            @pl.when(dest != v)
            def _():
                pix_copy(unit, dest, v).start()

    def group_at(step):
        return lax.rem(my_group + 1 + step, groups)

    one_unit(0, group_at(0), True)

    @pl.when(has_l)
    def _():
        halo_copy(0, halo_l, 0, 0, z - 1).wait_recv()

    @pl.when(has_r)
    def _():
        halo_copy(0, halo_r, 1, 1, z + 1).wait_recv()

    @pl.when(jnp.logical_not(has_l))
    def _():
        halo_l[...] = jnp.zeros_like(halo_l)

    @pl.when(jnp.logical_not(has_r))
    def _():
        halo_r[...] = jnp.zeros_like(halo_r)

    lax.fori_loop(0, visits, outer_band, 0, unroll=few)
    one_unit(1, group_at(0))

    def one_group(step, carry):
        for unit in range(UNITS):
            one_unit(unit, group_at(step))
        return carry

    lax.fori_loop(1, groups, one_group, 0)

    def weight_of(plane):
        plane = plane.astype(jnp.float32)
        positive = plane > 0
        return jnp.where(positive, 1.0 / jnp.where(positive, plane, 1.0), 0.0)

    own_first = pl.multiple_of((v - my_group * GROUP) * ROWS_DEV, ROWS_DEV)
    own_weight = weight_of(masked[rows_of(v), :])
    sums_ref[1] = own_weight

    def in_order(plane_of):
        lanes_of = {}
        for n, k in enumerate(order):
            part = plane_of(n // per_unit)
            at = n % per_unit * LANES
            lanes_of[k] = part[:, at : at + LANES]
        return jnp.concatenate([lanes_of[k] for k in range(blocks)], axis=1)

    sums_ref[0] = own_weight * in_order(lambda unit: total[unit, pl.ds(own_first, ROWS_DEV), :])

    def add_weight(step, carry):
        source = lax.rem(v + step, visits)
        var_copy(source, source).wait_recv()
        sums_ref[1] += weight_of(got_var[source])
        return carry

    lax.fori_loop(1, visits, add_weight, 0, unroll=few)

    base = my_group * GROUP

    def add_source(source):
        for unit in range(UNITS):
            pix_copy(unit, source, source).wait_recv()
        pixels = in_order(lambda unit: got_pix[unit, source]).astype(jnp.float32)
        sums_ref[0] += weight_of(got_var[source]) * pixels

    def add_far(step, carry):
        add_source(lax.rem(base + GROUP + step, visits))
        return carry

    def add_near(step, carry):
        add_source(base + lax.rem(v - base + step, GROUP))
        return carry

    lax.fori_loop(0, visits - GROUP, add_far, 0, unroll=few)
    lax.fori_loop(1, GROUP, add_near, 0, unroll=few)

    for step in range(1, visits):
        dest = lax.rem(v + step, visits)
        var_copy(dest, v).wait_send()
        for unit in range(UNITS):
            pix_copy(unit, dest, v).wait_send()

    @pl.when(has_l)
    def _():
        halo_copy(0, halo_r, 0, 1, z - 1).wait_send()

    @pl.when(has_r)
    def _():
        halo_copy(cols - LANES, halo_l, 1, 0, z + 1).wait_send()


def per_device(image, variance, mask_bits, boxes, row_filters, col_filters, coeffs):
    height, cols = image.shape[1], image.shape[2]
    visits, skies = lax.axis_size("visit"), lax.axis_size("sky")
    basis = row_filters.shape[0]
    blocks = cols // LANES
    span = cols // UNITS
    coeffs = jnp.transpose(coeffs, (2, 0, 1))
    hbm = pl.BlockSpec(memory_space=pltpu.HBM)
    f32, bf16 = jnp.float32, jnp.bfloat16
    dma = pltpu.SemaphoreType.DMA
    sums = pl.pallas_call(
        functools.partial(kernel, visits, skies),
        out_shape=jax.ShapeDtypeStruct((2, ROWS_DEV, cols), f32),
        in_specs=[hbm] * 7,
        out_specs=pl.BlockSpec(memory_space=pltpu.VMEM),
        scratch_shapes=[
            pltpu.VMEM(image.shape, bf16),
            pltpu.VMEM(variance.shape, bf16),
            pltpu.VMEM(mask_bits.shape, jnp.int32),
            pltpu.SMEM(boxes.shape, jnp.int32),
            pltpu.VMEM(row_filters.shape, bf16),
            pltpu.VMEM(col_filters.shape, bf16),
            pltpu.SMEM(coeffs.shape, f32),
            pltpu.VMEM((height, LANES), bf16),
            pltpu.VMEM((height, LANES), bf16),
            pltpu.VMEM((height, cols), bf16),
            pltpu.VMEM((visits, ROWS_DEV, cols), bf16),
            pltpu.VMEM((UNITS, height, span), bf16),
            pltpu.VMEM((UNITS, visits, ROWS_DEV, span), bf16),
            pltpu.VMEM((UNITS, BAND, span), f32),
            pltpu.VMEM((blocks, height + 2 * PAD, 2 * LANES), bf16),
            pltpu.VMEM((basis, BAND, WIN), bf16),
            pltpu.VMEM((basis, LANES, 2 * LANES), bf16),
            pltpu.VMEM((2, WIN, span), bf16),
            pltpu.VMEM((2, WIN, span), bf16),
            pltpu.VMEM((2, 24, WIN), f32),
            dma((7,)),
            dma((visits,)),
            dma((visits,)),
            dma((UNITS, visits)),
            dma((UNITS, visits)),
            dma((2,)),
            dma((2,)),
        ],
        compiler_params=pltpu.CompilerParams(
            collective_id=0, has_side_effects=True, vmem_limit_bytes=62 * 1024 * 1024
        ),
    )(image, variance, mask_bits, boxes, row_filters, col_filters, coeffs)
    return (sums[0] / jnp.maximum(sums[1], 1.0), sums[1])


def solution(mesh):
    in_specs = (
        P("visit", None, "sky"),
        P("visit", None, "sky"),
        P("visit", None, "sky"),
        P("visit", None),
        P(),
        P(),
        P("visit", None, None),
    )
    out_specs = (P("visit", "sky"), P("visit", "sky"))
    return jax.shard_map(
        per_device, mesh=mesh, in_specs=in_specs, out_specs=out_specs, check_vma=False
    )
```
